128 devices in a mesh: blk: 16 (over x, y_lo, core), grp: 8 (over z, y_hi).
Axes of the slice: x: 4, y: 4 (y_hi: 2, y_lo: 2; y = y_hi * 2 + y_lo), z: 4, core: 2. Of those that a mesh axis runs over, the one named last changes fastest.
Arguments:
- hidden: bfloat16 [131072, 2048], P(('blk', 'grp')), may hold values from -24 to 24
- weight: bfloat16 [2048, 512], replicated, may hold values from -0.125 to 0.125
- stamps: int32 [131072], P(('blk', 'grp')), may hold values from 0 to 511
- group_ids: int32 [131072], P(('blk', 'grp')), may hold values from 0 to 255
Outputs:
- grad_hidden: bfloat16 [131072, 2048], P(('blk', 'grp'))
- grad_weight: float32 [2048, 512], P(('blk', 'grp'))
- loss: float32 [], replicated
The draws below stay inside these ranges and needn't reach their ends.
All inputs are finite; a program needn't handle non-finite values.
Results may differ from the reference program's by a relative error of at most 0.0065.
Values may be sent and summed in bfloat16 or wider, within the bound.
A program may use at most 64 MiB of HBM per device.

```python
import math
import jax
import jax.numpy as jnp
from jax import lax

D = 512
FF = 2048
ROWS = 1024
TAU = 64
BUCKETS = 512
IDS = 256
ITEMS = 131072
PAIRS = 268369920
N_BLK = 16
N_GRP = 8


def draw_stamps(key, part):
    key = jax.random.fold_in(key, 11)
    block_count = ITEMS // ROWS
    position = jnp.arange(ITEMS, dtype=jnp.int32)
    block_id = position // ROWS
    spread = 32 + (BUCKETS - 32) * block_id // max(block_count - 1, 1)
    raw_bits = jax.random.randint(key, (ITEMS,), 0, 1 << 20, dtype=jnp.int32)
    stamp_value = raw_bits % spread
    inner = position % ROWS
    stamp_value = jnp.where(inner == 0, spread - 1, stamp_value)
    stamp_value = jnp.where(inner == 1, 0, stamp_value)
    return stamp_value.astype(jnp.int32)


def with_ends(values, rng, least, largest):
    longest = values.shape.index(max(values.shape))
    spots = []
    for shift in (0, 1):
        where = [jax.random.randint(jax.random.fold_in(rng, axis), (), 0, length) for axis, length in enumerate(values.shape)]
        where[longest] = (where[longest] + shift) % values.shape[longest]
        spots.append(tuple(where))
    return values.at[spots[0]].set(least).at[spots[1]].set(largest)


def with_spikes(result, stream_key, source, target, blocks, factor):
    owner, partner = [(jnp.arange(result.shape[axis_at]) // (result.shape[axis_at] // blocks)).reshape([-1 if axis == axis_at else 1 for axis in range(result.ndim)]) for axis_at in (source, target)]
    chosen = jax.random.permutation(stream_key, blocks)[partner]
    strong = (owner == chosen) | (owner == (partner + blocks // 2) % blocks)
    return jnp.where(strong, factor * result, result)


def block_levels(stream_key, extent, shards, smallest, largest):
    factor_of = 1.0
    for axis_at, blocks in shards:
        heights = jax.random.uniform(jax.random.fold_in(jax.random.fold_in(stream_key, 6), axis_at), (blocks,), jnp.float32, smallest / len(shards), largest / len(shards))
        factor_of = factor_of * jnp.repeat(jnp.exp(heights), extent[axis_at] // blocks).reshape((-1,) + (1,) * (len(extent) - 1 - axis_at))
    return factor_of


def normal_values(stream_key, dims, scale, bound, pieces=(), held_as=jnp.bfloat16):
    array = scale * jax.random.normal(stream_key, dims, jnp.float32)
    if pieces:
        array = array * block_levels(stream_key, dims, pieces, -0.22, 0.18)
    return jnp.clip(array, -bound, bound).astype(held_as)


def heavy_noise(rng, extent, scale, most, cuts, heavy, held_as=jnp.bfloat16):
    result = scale * jax.random.normal(rng, extent, jnp.float32)
    if cuts:
        result = result * block_levels(rng, extent, cuts, -0.22, 0.18)
    return jnp.clip(with_spikes(result, jax.random.fold_in(rng, 3), *heavy), -most, most).astype(held_as)


def setup_inputs(seed: int = 0) -> dict:
    key_list = jax.random.split(jax.random.key(seed), 5)
    hidden = heavy_noise(key_list[0], (ITEMS, FF), 1.0, 24.0, ((0, 128),), (0, 1, 128, 5.5))
    weight = normal_values(key_list[1], (FF, D), FF ** -0.5, 0.125)
    stamps = draw_stamps(jax.random.fold_in(key_list[4], 71), 0)
    group_ids = with_ends(jax.random.randint(key_list[3], (ITEMS,), 0, IDS), jax.random.fold_in(key_list[3], 1), 0, IDS - 1).astype(jnp.int32)
    return {"hidden": hidden, "weight": weight, "stamps": stamps, "group_ids": group_ids}


def pair_terms(left_emb, left_stamp, left_ids, right_emb, right_stamp, right_ids, keep_mask):
    inv_root = 1.0 / math.sqrt(D)
    scores = jnp.dot(left_emb, right_emb.T, preferred_element_type=jnp.float32) * inv_root
    gap_size = jnp.abs(left_stamp[:, None] - right_stamp[None, :]).astype(jnp.float32)
    pair_weights = jnp.exp(-gap_size / TAU) * keep_mask
    label_sign = jnp.where(left_ids[:, None] == right_ids[None, :], 1.0, -1.0).astype(jnp.float32)
    margin = -label_sign * scores
    losses = pair_weights * jax.nn.softplus(margin)
    coefficient = (pair_weights * -label_sign * jax.nn.sigmoid(margin) * inv_root).astype(jnp.bfloat16)
    return (coefficient, pair_weights, losses)

def reference(hidden, weight, stamps, group_ids):
    block_count = ITEMS // ROWS
    hidden_blocks = hidden.reshape(block_count, ROWS, FF)
    emb_blocks = lax.map(lambda block_rows: jnp.dot(block_rows, weight, preferred_element_type=jnp.float32).astype(jnp.bfloat16), hidden_blocks)
    stamp_blocks = stamps.reshape(block_count, ROWS)
    id_blocks = group_ids.reshape(block_count, ROWS)
    row_index = jnp.arange(ROWS, dtype=jnp.int32)
    offdiag = (row_index[:, None] != row_index[None, :]).astype(jnp.float32)
    round_masks = [N_GRP, N_GRP // 2, N_GRP * N_BLK // 2]

    def one_block(block_id):
        own_emb = emb_blocks[block_id]
        own_stamp = stamp_blocks[block_id]
        own_ids = id_blocks[block_id]
        coefficient, pair_weights, losses = pair_terms(own_emb, own_stamp, own_ids, own_emb, own_stamp, own_ids, offdiag)
        accum = jnp.dot(coefficient, own_emb, preferred_element_type=jnp.float32)
        weight_sum = 0.5 * jnp.sum(pair_weights)
        loss_sum = 0.5 * jnp.sum(losses)
        for round_mask in round_masks:
            partner = jnp.bitwise_xor(block_id, round_mask).astype(jnp.int32)
            other_emb = emb_blocks[partner]
            coefficient, pair_weights, losses = pair_terms(own_emb, own_stamp, own_ids, other_emb, stamp_blocks[partner], id_blocks[partner], jnp.float32(1.0))
            accum = accum + jnp.dot(coefficient, other_emb, preferred_element_type=jnp.float32)
            weight_sum = weight_sum + 0.5 * jnp.sum(pair_weights)
            loss_sum = loss_sum + 0.5 * jnp.sum(losses)
        return (accum.astype(jnp.bfloat16), weight_sum, loss_sum)
    summed_blocks, weight_sums, loss_sums = lax.map(one_block, jnp.arange(block_count, dtype=jnp.int32))
    weight_total = jnp.sum(weight_sums)
    pair_loss = jnp.sum(loss_sums)
    loss = pair_loss / weight_total
    mean_weight = weight_total / PAIRS
    grad_hidden = lax.map(lambda block_grad: (jnp.dot(block_grad, weight.T, preferred_element_type=jnp.float32) / mean_weight).astype(jnp.bfloat16), summed_blocks).reshape(ITEMS, FF)
    summed = summed_blocks.reshape(ITEMS, D)
    grad_weight = lax.dot_general(hidden, summed, (((0,), (0,)), ((), ())), preferred_element_type=jnp.float32) / (mean_weight * ITEMS)
    return (grad_hidden, grad_weight, loss)
```

```python
import functools
import math

import jax
import jax.numpy as jnp
from jax import lax
from jax.experimental import pallas as pl
from jax.experimental.pallas import tpu as pltpu
from jax.sharding import PartitionSpec as P

ROWS = 1024
FF = 2048
D = 512
TAU = 64
CHUNK = 256
MESH = pl.DeviceIdType.MESH
NT = (((1,), (1,)), ((), ()))
SCALE2 = math.log2(math.e) / math.sqrt(D)
ORDERS = ("xyz", "yzx", "zxy", "xzy")


def place(x, y, z, c):
    return (x * 4 + (y % 2) * 2 + c, z * 2 + y // 2)


def kernel(
    hidden_hbm, weight_hbm, stamps_ref, ids_ref,
    gh_hbm, gw_ref, tot_ref,
    hid, wgt, ht, emb, mate, zx, aux, theirs, col_u, col_v, col_i, row_u, row_v, row_i,
    acc, summed, coef, sums, psend, precv, part1, part2, part3, got1, got2, got3,
    tsend, tcore, taxis, ghs,
    in_sem, out_sem, aux_send, aux_recv, core_send, core_recv, zx_send, zx_recv,
    p_send, p_recv, s1_send, s1_recv, s2_send, s2_recv, s3_send, s3_recv,
    tc_send, tc_recv, ta_send, ta_recv,
):
    b = lax.axis_index("blk")
    g = lax.axis_index("grp")
    at = {"x": b // 4, "y": (g % 2) * 2 + (b // 2) % 2, "z": g // 2}
    core = b % 2

    def peer(axis, ahead):
        there = dict(at)
        there[axis] = (at[axis] + ahead) % 4
        return place(there["x"], there["y"], there["z"], core)

    core_mate = place(at["x"], at["y"], at["z"], 1 - core)
    partners = (core_mate, peer("z", 2), peer("x", 2))

    def remote(src, dst, send, recv, device):
        return pltpu.make_async_remote_copy(
            src_ref=src, dst_ref=dst, send_sem=send, recv_sem=recv,
            device_id=device, device_id_type=MESH,
        )

    def weight_in():
        return pltpu.make_async_copy(weight_hbm, wgt, in_sem.at[4])

    def hidden_in(i):
        rows = pl.ds(i * CHUNK, CHUNK)
        return pltpu.make_async_copy(hidden_hbm.at[rows], hid.at[rows], in_sem.at[i])

    def grad_out(i):
        rows = pl.ds(i * CHUNK, CHUNK)
        return pltpu.make_async_copy(ghs.at[rows], gh_hbm.at[rows], out_sem.at[i])

    def aux_copy(k):
        return remote(aux, theirs.at[k], aux_send.at[k], aux_recv.at[k], partners[k])

    def core_copy(i):
        rows = pl.ds(i * CHUNK, CHUNK)
        return remote(emb.at[rows], mate.at[rows], core_send.at[i], core_recv.at[i], core_mate)

    def zx_copy(i, k):
        return remote(
            emb.at[pl.ds(i * 128, 128)], zx.at[i, pl.ds(k * 128, 128)],
            zx_send.at[k, i], zx_recv.at[k, i], partners[1 + k],
        )

    def p_copy(i):
        return remote(psend.at[i], precv.at[i], p_send.at[i], p_recv.at[i], core_mate)

    def stage_copy(p, stage, ahead):
        axis = ORDERS[p][stage]
        src, dst, send, recv = (
            (part1, got1, s1_send, s1_recv),
            (part2, got2, s2_send, s2_recv),
            (part3, got3, s3_send, s3_recv),
        )[stage]
        return remote(
            src.at[p, (at[axis] + ahead) % 4], dst.at[p, ahead - 1],
            send.at[p, ahead - 1], recv.at[p, ahead - 1], peer(axis, ahead),
        )

    def total_core():
        return remote(tsend.at[0], tcore, tc_send, tc_recv, core_mate)

    def total_axis(n, ahead):
        axis = "xyz"[n]
        return remote(
            tsend.at[1 + n], taxis.at[n, at[axis]],
            ta_send.at[n, ahead - 1], ta_recv.at[n, ahead - 1], peer(axis, ahead),
        )

    hidden_in(0).start()
    weight_in().start()
    for i in range(1, 4):
        hidden_in(i).start()

    barrier = pltpu.get_barrier_semaphore()
    pl.semaphore_signal(barrier, inc=1, device_id=core_mate, device_id_type=MESH)
    for axis in "xyz":
        for ahead in (1, 2, 3):
            pl.semaphore_signal(barrier, inc=1, device_id=peer(axis, ahead), device_id_type=MESH)

    aux[0] = stamps_ref[...]
    aux[1] = ids_ref[...]

    def columns(k, stamps, ids):
        times = stamps.astype(jnp.float32) * (1.0 / TAU)
        u = jnp.exp(times)
        v = jnp.exp(-times)
        names = ids.astype(jnp.float32)
        col_u[k] = u
        col_v[k] = v
        col_i[k] = names
        return u, v, names

    u, v, names = columns(0, stamps_ref[...], ids_ref[...])
    root = 1.0 / math.sqrt(D)
    for value, rows in zip((u * root, v * root, names), (row_u, row_v, row_i)):
        for r in range(8):
            rows[r * 128 : (r + 1) * 128, :] = jnp.broadcast_to(value[r : r + 1, :], (128, 128)).T
    acc[...] = jnp.zeros_like(acc)
    sums[...] = jnp.zeros_like(sums)

    pl.semaphore_wait(barrier, 10)
    for k in range(3):
        aux_copy(k).start()
    weight_in().wait()

    def embed(i, carry):
        hidden_in(i).wait()
        rows = pl.ds(pl.multiple_of(i * CHUNK, CHUNK), CHUNK)
        emb[rows, :] = jnp.dot(
            hid[rows, :], wgt[...], preferred_element_type=jnp.float32
        ).astype(jnp.bfloat16)
        for h in range(2):
            for k in range(2):
                zx_copy(2 * i + h, k).start()
        core_copy(i).start()
        return carry

    lax.fori_loop(0, 4, embed, 0)

    def pairs(other, cols, diagonal=None):
        loss = jnp.zeros((8, 128), jnp.float32)
        total = jnp.zeros((8, 128), jnp.float32)
        for r in range(4):
            s = lax.dot_general(
                emb[r * CHUNK : (r + 1) * CHUNK, :], other, NT,
                preferred_element_type=jnp.float32,
            )
            for q in range(8):
                lo = r * CHUNK + q * 32
                ru, rv, ri = row_u[lo : lo + 32, :], row_v[lo : lo + 32, :], row_i[lo : lo + 32, :]
                for h in range(2):
                    cu, cv, ci = cols[h]
                    p = s[q * 32 : (q + 1) * 32, h * 128 : (h + 1) * 128] * SCALE2
                    w = jnp.minimum(ru * cv, rv * cu)
                    if diagonal is not None:
                        i = lax.broadcasted_iota(jnp.int32, (32, 128), 0) + lo
                        j = lax.broadcasted_iota(jnp.int32, (32, 128), 1) + (diagonal + h * 128)
                        w = jnp.where(i == j, 0.0, w)
                    same = ri == ci
                    minus = -p
                    e = jnp.exp2(jnp.minimum(p, minus))
                    t = 1.0 + e
                    m = jnp.where(same, minus, p)
                    sig = pl.reciprocal(t, approx=True) * jnp.where(m >= 0.0, 1.0, e)
                    c = w * sig
                    c = jnp.where(same, -c, c)
                    coef[r, q * 32 : (q + 1) * 32, h * 128 : (h + 1) * 128] = c.astype(jnp.bfloat16)
                    term = w * (jnp.maximum(m, 0.0) + jnp.log2(t))
                    for n in range(4):
                        loss = loss + term[n * 8 : (n + 1) * 8]
                        total = total + w[n * 8 : (n + 1) * 8]
            acc[r * CHUNK : (r + 1) * CHUNK, :] += jnp.dot(
                coef[r], other, preferred_element_type=jnp.float32
            )
        sums[0] += total
        sums[1] += loss

    def col_of(k, i):
        return tuple(ref[k, pl.ds(i, 1), :] for ref in (col_u, col_v, col_i))

    def own_step(i, carry):
        rows = pl.ds(pl.multiple_of(i * CHUNK, CHUNK), CHUNK)
        pairs(emb[rows, :], (col_of(0, 2 * i), col_of(0, 2 * i + 1)), i * CHUNK)
        return carry

    lax.fori_loop(0, 4, own_step, 0)

    for k in range(3):
        aux_copy(k).wait_recv()
        columns(1 + k, theirs[k, 0], theirs[k, 1])

    def core_step(i, carry):
        core_copy(i).wait_recv()
        rows = pl.ds(pl.multiple_of(i * CHUNK, CHUNK), CHUNK)
        pairs(mate[rows, :], (col_of(1, 2 * i), col_of(1, 2 * i + 1)))
        return carry

    lax.fori_loop(0, 4, core_step, 0)

    def zx_step(i, carry):
        for c in range(2):
            lanes = pl.ds(pl.multiple_of(i * 256 + c * 128, 128), 128)
            turned = hid[:, lanes].T
            for n in range(8):
                ht[c, i // 2, (n % 2) * 2 + i % 2, n // 2] = turned[n * 16 : (n + 1) * 16, :]
        for k in range(2):
            zx_copy(i, k).wait_recv()
        pairs(zx[i], (col_of(2, i), col_of(3, i)))
        return carry

    lax.fori_loop(0, 8, zx_step, 0)

    summed[...] = acc[...].astype(jnp.bfloat16)

    def p_other(i, carry):
        block = ht[1 - core, i].reshape(CHUNK, ROWS)
        psend[i] = (
            jnp.dot(block, summed[...], preferred_element_type=jnp.float32)
            .astype(jnp.bfloat16)
            .reshape(4, 4, 16, D)
        )
        p_copy(i).start()
        return carry

    lax.fori_loop(0, 4, p_other, 0)

    line = lax.broadcasted_iota(jnp.int32, (8, 128), 0)
    w_sum = jnp.sum(sums[0], axis=0, keepdims=True)
    l_sum = jnp.sum(sums[1], axis=0, keepdims=True)
    tsend[0] = jnp.where(line == 0, w_sum, jnp.where(line == 1, l_sum, 0.0))
    total_core().start()

    def p_own(i, carry):
        block = ht[core, i].reshape(CHUNK, ROWS)
        v = jnp.dot(block, summed[...], preferred_element_type=jnp.float32)
        p_copy(i).wait_recv()
        v = v + precv[i].reshape(CHUNK, D).astype(jnp.float32)
        v = v.astype(jnp.bfloat16).reshape(4, 4, 16, D)
        part1[0, i] = v[..., :128]
        part1[1, :, :, i] = v[..., 128:256]
        for y in range(4):
            part1[2, :, i, y] = v[y, :, :, 256:384]
            part1[3, i, :, y] = v[y, :, :, 384:]
        return carry

    lax.fori_loop(0, 4, p_own, 0)

    for p in range(4):
        for ahead in (2, 1, 3):
            stage_copy(p, 0, ahead).start()
    total_core().wait_recv()

    def spread(n, value):
        tsend[1 + n] = value
        taxis[n, at["xyz"[n]]] = value
        for ahead in (2, 1, 3):
            total_axis(n, ahead).start()

    def gathered(n):
        for ahead in (1, 2, 3):
            total_axis(n, ahead).wait_recv()
        return (taxis[n, 0] + taxis[n, 1]) + (taxis[n, 2] + taxis[n, 3])

    spread(0, tsend[0] + tcore[...])

    def grad_rows(i, carry):
        rows = pl.ds(pl.multiple_of(i * CHUNK, CHUNK), CHUNK)
        for n in range(4):
            ghs[rows, n * 512 : (n + 1) * 512] = lax.dot_general(
                summed[rows, :], wgt[n * 512 : (n + 1) * 512, :], NT,
                preferred_element_type=jnp.float32,
            ).astype(jnp.bfloat16)
        grad_out(i).start()
        return carry

    lax.fori_loop(0, 2, grad_rows, 0)

    def reduced(p, stage):
        src, got = ((part1, got1), (part2, got2), (part3, got3))[stage]
        for ahead in (1, 2, 3):
            stage_copy(p, stage, ahead).wait_recv()
        v = src[p, at[ORDERS[p][stage]]].astype(jnp.float32)
        for n in range(3):
            v = v + got[p, n].astype(jnp.float32)
        return v

    for p in (1, 2, 0, 3):
        part2[p] = reduced(p, 0).astype(jnp.bfloat16)
        for ahead in (2, 1, 3):
            stage_copy(p, 1, ahead).start()
    spread(1, gathered(0))

    lax.fori_loop(2, 3, grad_rows, 0)

    for p in range(4):
        part3[p] = reduced(p, 1).astype(jnp.bfloat16)
        for ahead in (2, 1, 3):
            stage_copy(p, 2, ahead).start()
    spread(2, gathered(1))

    lax.fori_loop(3, 4, grad_rows, 0)

    for p in range(4):
        gw_ref[:, p * 128 : (p + 1) * 128] = reduced(p, 2)
    tot_ref[...] = jnp.broadcast_to(
        jnp.sum(gathered(2), axis=1, keepdims=True), (8, 128)
    )

    for k in range(3):
        aux_copy(k).wait_send()
    for i in range(4):
        core_copy(i).wait_send()
        p_copy(i).wait_send()
        grad_out(i).wait()
    for i in range(8):
        for k in range(2):
            zx_copy(i, k).wait_send()
    total_core().wait_send()
    for ahead in (1, 2, 3):
        for p in range(4):
            for stage in range(3):
                stage_copy(p, stage, ahead).wait_send()
        for n in range(3):
            total_axis(n, ahead).wait_send()


def on_device(hidden, weight, stamps, group_ids):
    device_count = lax.axis_size("blk") * lax.axis_size("grp")
    bf, f32 = jnp.bfloat16, jnp.float32
    sem = pltpu.SemaphoreType.DMA
    vm = pltpu.VMEM
    whole = pl.BlockSpec(memory_space=pl.ANY)
    local = pl.BlockSpec(memory_space=pltpu.VMEM)
    grad, partial, totals = pl.pallas_call(
        kernel,
        out_shape=(
            jax.ShapeDtypeStruct((ROWS, FF), bf),
            jax.ShapeDtypeStruct((16, D), f32),
            jax.ShapeDtypeStruct((8, 128), f32),
        ),
        in_specs=[whole, whole, local, local],
        out_specs=(whole, local, local),
        scratch_shapes=[
            vm((ROWS, FF), bf), vm((FF, D), bf), vm((2, 4, 4, 4, 16, ROWS), bf),
            vm((ROWS, D), bf), vm((ROWS, D), bf), vm((8, CHUNK, D), bf),
            vm((2, 8, 128), jnp.int32), vm((3, 2, 8, 128), jnp.int32),
            vm((4, 8, 128), f32), vm((4, 8, 128), f32), vm((4, 8, 128), f32),
            vm((ROWS, 128), f32), vm((ROWS, 128), f32), vm((ROWS, 128), f32),
            vm((ROWS, D), f32), vm((ROWS, D), bf), vm((4, CHUNK, CHUNK), bf),
            vm((2, 8, 128), f32),
            vm((4, 4, 4, 16, D), bf), vm((4, 4, 4, 16, D), bf),
            vm((4, 4, 4, 4, 16, 128), bf), vm((4, 4, 4, 16, 128), bf), vm((4, 4, 16, 128), bf),
            vm((4, 3, 4, 4, 16, 128), bf), vm((4, 3, 4, 16, 128), bf), vm((4, 3, 16, 128), bf),
            vm((4, 8, 128), f32), vm((8, 128), f32), vm((3, 4, 8, 128), f32),
            vm((ROWS, FF), bf),
            sem((5,)), sem((4,)), sem((3,)), sem((3,)), sem((4,)), sem((4,)),
            sem((2, 8)), sem((2, 8)), sem((4,)), sem((4,)),
            sem((4, 3)), sem((4, 3)), sem((4, 3)), sem((4, 3)), sem((4, 3)), sem((4, 3)),
            sem, sem, sem((3, 3)), sem((3, 3)),
        ],
        compiler_params=pltpu.CompilerParams(
            collective_id=0, has_side_effects=True, vmem_limit_bytes=56 << 20
        ),
        cost_estimate=pl.CostEstimate(
            flops=15 * 10**9, bytes_accessed=11 << 20, transcendentals=12 << 20
        ),
    )(hidden, weight, stamps.reshape(8, 128), group_ids.reshape(8, 128))
    weight_total = (0.5 * math.sqrt(D)) * totals[0, 0]
    pair_loss = (0.5 * math.sqrt(D) * math.log(2.0)) * totals[1, 0]
    pair_count = (
        device_count * ROWS * (ROWS - 1) // 2 + 3 * device_count * ROWS * ROWS // 2
    )
    mean_weight = weight_total / float(pair_count)
    grad_hidden = (grad.astype(f32) / mean_weight).astype(bf)
    grad_weight = partial / (mean_weight * float(device_count * ROWS))
    return grad_hidden, grad_weight, pair_loss / weight_total


def solution(mesh):
    in_specs = (P(("blk", "grp"), None), P(), P(("blk", "grp")), P(("blk", "grp")))
    out_specs = (P(("blk", "grp"), None), P(("blk", "grp"), None), P())
    return jax.shard_map(
        on_device, mesh=mesh, in_specs=in_specs, out_specs=out_specs, check_vma=False
    )
```

```python
import functools
import math

import jax
import jax.numpy as jnp
from jax import lax
from jax.experimental import pallas as pl
from jax.experimental.pallas import tpu as pltpu
from jax.sharding import PartitionSpec as P

ROWS = 1024
FF = 2048
D = 512
TAU = 64
CHUNK = 256
MESH = pl.DeviceIdType.MESH
NT = (((1,), (1,)), ((), ()))
SCALE2 = math.log2(math.e) / math.sqrt(D)
ORDERS = ("xyz", "yzx", "zxy", "mzn")


def place(x, y, z, c):
    return (x * 4 + (y % 2) * 2 + c, z * 2 + y // 2)


def kernel(
    hidden_hbm, weight_hbm, stamps_hbm, ids_hbm,
    gh_ref, gw_ref, tot_ref,
    hid, wgt, ht, htm, emb, aux, theirs, col_u, col_v, col_i, row_u, row_v, row_i,
    acc, summed, coef, coef_last, sums, pown, part1, part2, part3, got1, got2, got3,
    tsend, tcore, taxis,
    in_sem, aux_send, aux_recv, core_send, core_recv, zx_send, zx_recv,
    h_send, h_recv, p_send, p_recv, s1_send, s1_recv, s2_send, s2_recv, s3_send, s3_recv,
    tc_send, tc_recv, ta_send, ta_recv,
):
    b = lax.axis_index("blk")
    g = lax.axis_index("grp")
    at = {"x": b // 4, "y": (g % 2) * 2 + (b // 2) % 2, "z": g // 2}
    core = b % 2

    at["m"] = at["x"] * (1 - core) + at["y"] * core
    at["n"] = at["y"] * (1 - core) + at["x"] * core

    def peer(axis, ahead):
        steps = {
            "x": (ahead, 0, 0), "y": (0, ahead, 0), "z": (0, 0, ahead),
            "m": (ahead * (1 - core), ahead * core, 0),
            "n": (ahead * core, ahead * (1 - core), 0),
        }[axis]
        there = [(at[a] + step) % 4 for a, step in zip("xyz", steps)]
        return place(*there, core)

    core_mate = place(at["x"], at["y"], at["z"], 1 - core)
    partners = (core_mate, peer("z", 2), peer("x", 2))

    def remote(src, dst, send, recv, device):
        return pltpu.make_async_remote_copy(
            src_ref=src, dst_ref=dst, send_sem=send, recv_sem=recv,
            device_id=device, device_id_type=MESH,
        )

    def weight_in():
        return pltpu.make_async_copy(weight_hbm, wgt, in_sem.at[8])

    def hidden_in(i):
        rows = pl.ds(i * 128, 128)
        return pltpu.make_async_copy(hidden_hbm.at[rows], hid.at[rows], in_sem.at[i])

    def aux_in(k):
        return pltpu.make_async_copy((stamps_hbm, ids_hbm)[k], aux.at[k], in_sem.at[9 + k])

    def aux_copy(k):
        return remote(aux, theirs.at[k], aux_send.at[k], aux_recv.at[k], partners[k])

    def core_copy(i):
        return remote(
            emb.at[pl.ds(i * CHUNK, CHUNK)], emb.at[pl.ds(ROWS + i * CHUNK, CHUNK)],
            core_send.at[i], core_recv.at[i], core_mate,
        )

    def zx_copy(i, k):
        return remote(
            emb.at[pl.ds(i * 128, 128)], emb.at[pl.ds(2 * ROWS + i * CHUNK + k * 128, 128)],
            zx_send.at[k, i], zx_recv.at[k, i], partners[1 + k],
        )

    def h_copy(i):
        return remote(ht.at[1 - core, i], htm.at[i], h_send.at[i], h_recv.at[i], core_mate)

    def p_copy(i):
        rows = pl.ds(i * CHUNK, CHUNK)
        return remote(
            summed.at[0, rows], summed.at[1, rows], p_send.at[i], p_recv.at[i], core_mate
        )

    def stage_copy(p, stage, ahead):
        axis = ORDERS[p][stage]
        src, dst, send, recv = (
            (part1, got1, s1_send, s1_recv),
            (part2, got2, s2_send, s2_recv),
            (part3, got3, s3_send, s3_recv),
        )[stage]
        return remote(
            src.at[p, (at[axis] + ahead) % 4], dst.at[p, ahead - 1],
            send.at[p, ahead - 1], recv.at[p, ahead - 1], peer(axis, ahead),
        )

    def total_core():
        return remote(tsend.at[0], tcore, tc_send, tc_recv, core_mate)

    def total_axis(n, ahead):
        axis = "xyz"[n]
        return remote(
            tsend.at[1 + n], taxis.at[n, at[axis]],
            ta_send.at[n, ahead - 1], ta_recv.at[n, ahead - 1], peer(axis, ahead),
        )

    for k in range(2):
        aux_in(k).start()
    weight_in().start()
    for i in range(8):
        hidden_in(i).start()

    barrier = pltpu.get_barrier_semaphore()
    pl.semaphore_signal(barrier, inc=1, device_id=core_mate, device_id_type=MESH)
    for axis in "zxy":
        for ahead in (2, 1, 3):
            pl.semaphore_signal(barrier, inc=1, device_id=peer(axis, ahead), device_id_type=MESH)

    weight_in().wait()

    def embed(first, count):
        for n in range(count // 128):
            hidden_in(first // 128 + n).wait()
        rows = pl.ds(first, count)
        emb[rows, :] = jnp.dot(
            hid[rows, :], wgt[...], preferred_element_type=jnp.float32
        ).astype(jnp.bfloat16)

    embed(0, 128)
    pl.semaphore_wait(barrier, 10)
    for k in range(2):
        zx_copy(0, k).start()
    for k in range(2):
        aux_in(k).wait()
    for k in range(3):
        aux_copy(k).start()
    embed(128, 128)
    for k in range(2):
        zx_copy(1, k).start()
    core_copy(0).start()

    def embed_rest(i, carry):
        embed(pl.multiple_of(i * CHUNK, CHUNK), CHUNK)
        for h in range(2):
            for k in range(2):
                zx_copy(2 * i + h, k).start()
        core_copy(i).start()
        return carry

    lax.fori_loop(1, 4, embed_rest, 0)

    def columns(place_of, stamps, ids):
        times = stamps.astype(jnp.float32) * (1.0 / TAU)
        values = (jnp.exp(times), jnp.exp(-times), ids.astype(jnp.float32))
        for value, ref in zip(values, (col_u, col_v, col_i)):
            for r in range(8):
                ref[place_of(r) : place_of(r) + 1, :] = value[r : r + 1, :]
        return values

    u, v, names = columns(lambda r: r, aux[0], aux[1])
    ln2 = math.log(2.0)
    for value, rows in zip((u * ln2, v * ln2, names), (row_u, row_v, row_i)):
        for r in range(8):
            rows[r * 128 : (r + 1) * 128, :] = jnp.broadcast_to(value[r : r + 1, :], (128, 128)).T
    acc[...] = jnp.zeros_like(acc)
    sums[...] = jnp.zeros_like(sums)

    def pairs(first, width, coef, diagonal=False, last=False):
        other = emb[pl.ds(pl.multiple_of(first, width), width), :]
        cols = [
            [ref[pl.ds(first // 128 + h, 1), :] for ref in (col_u, col_v, col_i)]
            for h in range(width // 128)
        ]
        loss = jnp.zeros((8, 128), jnp.float32)
        total = jnp.zeros((8, 128), jnp.float32)

        def scores(r):
            return lax.dot_general(
                emb[r * CHUNK : (r + 1) * CHUNK, :], other, NT,
                preferred_element_type=jnp.float32,
            )

        def gather(r):
            rows = slice(r * CHUNK, (r + 1) * CHUNK)
            v = acc[rows, :] + jnp.dot(coef[rows, :], other, preferred_element_type=jnp.float32)
            if last:
                summed[0, rows, :] = v.astype(jnp.bfloat16)
                p_copy(r).start()
            else:
                acc[rows, :] = v

        s = scores(0)
        for r in range(4):
            s_next = scores(r + 1) if r < 3 else None
            if r > 0:
                gather(r - 1)
            for q in range(8):
                lo = r * CHUNK + q * 32
                ru, rv, ri = row_u[lo : lo + 32, :], row_v[lo : lo + 32, :], row_i[lo : lo + 32, :]
                for h in range(width // 128):
                    cu, cv, ci = cols[h]
                    sign = jnp.where(ri == ci, -SCALE2, SCALE2)
                    m = s[q * 32 : (q + 1) * 32, h * 128 : (h + 1) * 128] * sign
                    plus = jnp.maximum(m, jnp.log2(1.0 + jnp.exp2(jnp.minimum(m, 100.0))))
                    w = jnp.minimum(ru * cv, rv * cu)
                    if diagonal:
                        i = lax.broadcasted_iota(jnp.int32, (32, 128), 0) + lo
                        j = lax.broadcasted_iota(jnp.int32, (32, 128), 1) + (first + h * 128)
                        w = jnp.where(i == j, 0.0, w)
                    c = (w * sign) * jnp.exp2(m - plus)
                    coef[lo : lo + 32, h * 128 : (h + 1) * 128] = c.astype(jnp.bfloat16)
                    term = w * plus
                    for n in range(4):
                        loss = loss + term[n * 8 : (n + 1) * 8]
                        total = total + w[n * 8 : (n + 1) * 8]
            s = s_next
        gather(3)
        sums[0] += total
        sums[1] += loss

    def own_step(i, carry):
        pairs(i * 512, 512, coef, True)
        return carry

    lax.fori_loop(0, 2, own_step, 0)

    for k in range(3):
        aux_copy(k).wait_recv()
    columns(lambda r: 8 + r, theirs[0, 0], theirs[0, 1])
    columns(lambda r: 16 + 2 * r, theirs[1, 0], theirs[1, 1])
    columns(lambda r: 17 + 2 * r, theirs[2, 0], theirs[2, 1])

    def turn(x, carry):
        for n in range(4):
            lanes = pl.ds(pl.multiple_of(x * 512 + n * 128, 128), 128)
            turned = hid[:, lanes].T
            for k in range(8):
                ht[n % 2, x, (k % 2) * 2 + n // 2, k // 2] = turned[k * 16 : (k + 1) * 16, :]
        h_copy(x).start()
        return carry

    def other_step(i, carry):
        @pl.when(i < 2)
        def _():
            for n in range(2):
                core_copy(2 * i + n).wait_recv()

        @pl.when(i == 2)
        def _():
            lax.fori_loop(0, 4, turn, 0)

        @pl.when(i >= 2)
        def _():
            for n in range(2):
                for k in range(2):
                    zx_copy(2 * (i - 2) + n, k).wait_recv()

        pairs(ROWS + i * 512, 512, coef)
        return carry

    lax.fori_loop(0, 5, other_step, 0)

    for i in (6, 7):
        for k in range(2):
            zx_copy(i, k).wait_recv()
        pairs(2 * ROWS + i * CHUNK, CHUNK, coef_last, last=i == 7)

    line = lax.broadcasted_iota(jnp.int32, (8, 128), 0)
    w_sum = jnp.sum(sums[0], axis=0, keepdims=True)
    l_sum = jnp.sum(sums[1], axis=0, keepdims=True)
    tsend[0] = jnp.where(line == 0, w_sum, jnp.where(line == 1, l_sum, 0.0))
    total_core().start()

    def own_half(x, carry):
        block = ht[core, x].reshape(CHUNK, ROWS)
        pown[x] = jnp.dot(block, summed[0], preferred_element_type=jnp.float32)
        return carry

    lax.fori_loop(0, 4, own_half, 0)
    for i in range(4):
        h_copy(i).wait_recv()
        p_copy(i).wait_recv()

    def mate_half(pair):
        lanes = slice(pair * 256, (pair + 1) * 256)

        def step(x, carry):
            block = htm[x].reshape(CHUNK, ROWS)
            v = pown[x, :, lanes] + jnp.dot(
                block, summed[1, :, lanes], preferred_element_type=jnp.float32
            )
            v = v.astype(jnp.bfloat16).reshape(4, 4, 16, 256)
            if pair == 0:
                part1[0, x] = v[..., :128]
                part1[1, :, :, x] = v[..., 128:]
            else:
                for y in range(4):
                    part1[2, :, x, y] = v[y, :, :, :128]
                    m = x * (1 - core) + y * core
                    n = y * (1 - core) + x * core
                    part1[3, m, :, n] = v[y, :, :, 128:]
            return carry

        lax.fori_loop(0, 4, step, 0)
        for p in (2 * pair, 2 * pair + 1):
            for ahead in (2, 1, 3):
                stage_copy(p, 0, ahead).start()

    mate_half(0)
    mate_half(1)
    total_core().wait_recv()

    def spread(n, value):
        tsend[1 + n] = value
        taxis[n, at["xyz"[n]]] = value
        for ahead in (2, 1, 3):
            total_axis(n, ahead).start()

    def gathered(n):
        for ahead in (1, 2, 3):
            total_axis(n, ahead).wait_recv()
        return (taxis[n, 0] + taxis[n, 1]) + (taxis[n, 2] + taxis[n, 3])

    spread(0, tsend[0] + tcore[...])

    def grad_rows(i, carry):
        rows = pl.ds(pl.multiple_of(i * CHUNK, CHUNK), CHUNK)
        for n in range(4):
            gh_ref[rows, n * 512 : (n + 1) * 512] = lax.dot_general(
                summed[0, rows, :], wgt[n * 512 : (n + 1) * 512, :], NT,
                preferred_element_type=jnp.float32,
            ).astype(jnp.bfloat16)
        return carry

    lax.fori_loop(0, 4, grad_rows, 0)

    for k in range(3):
        aux_copy(k).wait_send()
    for i in range(4):
        core_copy(i).wait_send()
        h_copy(i).wait_send()
        p_copy(i).wait_send()
    for i in range(8):
        for k in range(2):
            zx_copy(i, k).wait_send()
    total_core().wait_send()

    def sent(stage):
        for ahead in (1, 2, 3):
            for p in range(4):
                stage_copy(p, stage, ahead).wait_send()
            total_axis(stage, ahead).wait_send()

    def reduced(p, stage):
        src, got = ((part1, got1), (part2, got2), (part3, got3))[stage]
        for ahead in (1, 2, 3):
            stage_copy(p, stage, ahead).wait_recv()
        v = src[p, at[ORDERS[p][stage]]].astype(jnp.float32)
        for n in range(3):
            v = v + got[p, n].astype(jnp.float32)
        return v

    for p in range(4):
        part2[p] = reduced(p, 0).astype(jnp.bfloat16)
        for ahead in (2, 1, 3):
            stage_copy(p, 1, ahead).start()
    spread(1, gathered(0))
    sent(0)

    for p in range(4):
        part3[p] = reduced(p, 1).astype(jnp.bfloat16)
        for ahead in (2, 1, 3):
            stage_copy(p, 2, ahead).start()
    spread(2, gathered(1))
    sent(1)

    for p in range(4):
        gw_ref[:, p * 128 : (p + 1) * 128] = reduced(p, 2)
    tot_ref[...] = jnp.broadcast_to(
        jnp.sum(gathered(2), axis=1, keepdims=True), (8, 128)
    )

    for ahead in (1, 2, 3):
        for p in range(4):
            stage_copy(p, 2, ahead).wait_send()
        total_axis(2, ahead).wait_send()


def scale_kernel(pair_count, items, gh_ref, gw_ref, tot_ref, gh_out, gw_out, loss_out, buf, sem):
    scale = 1.0 / math.log(2.0)
    totals = tot_ref[...]
    weight_total = totals[0:1, :] * (0.5 * scale)
    pair_loss = totals[1:2, :] * 0.5
    inverse = float(pair_count) / weight_total
    across = jnp.broadcast_to(jnp.concatenate([inverse] * 16, axis=1), (8, FF))

    def out(i):
        rows = pl.ds(i * 128, 128)
        return pltpu.make_async_copy(buf.at[rows], gh_out.at[rows], sem.at[i])

    for i in range(8):
        for n in range(8):
            rows = slice(i * 128 + n * 16, i * 128 + (n + 1) * 16)
            v = gh_ref[rows, :].astype(jnp.float32) * jnp.concatenate([across] * 2, axis=0)
            buf[rows, :] = v.astype(jnp.bfloat16)
        out(i).start()
    gw_out[...] = gw_ref[...] * (across[0:1, :D] * (1.0 / items))
    loss_out[...] = (pair_loss / weight_total)[:, 0:1]
    for i in range(8):
        out(i).wait()


def on_device(hidden, weight, stamps, group_ids):
    device_count = lax.axis_size("blk") * lax.axis_size("grp")
    bf, f32 = jnp.bfloat16, jnp.float32
    sem = pltpu.SemaphoreType.DMA
    vm = pltpu.VMEM
    whole = pl.BlockSpec(memory_space=pl.ANY)
    outside = pl.BlockSpec(memory_space=pltpu.HBM)
    local = pl.BlockSpec(memory_space=pltpu.VMEM)
    grad, partial, totals = pl.pallas_call(
        kernel,
        out_shape=(
            pltpu.VMEM((ROWS, FF), bf),
            pltpu.VMEM((16, D), f32),
            pltpu.VMEM((8, 128), f32),
        ),
        in_specs=[outside] * 4,
        out_specs=(local, local, local),
        scratch_shapes=[
            vm((ROWS, FF), bf), vm((FF, D), bf), vm((2, 4, 4, 4, 16, ROWS), bf),
            vm((4, 4, 4, 16, ROWS), bf), vm((4 * ROWS, D), bf),
            vm((2, 8, 128), jnp.int32), vm((3, 2, 8, 128), jnp.int32),
            vm((32, 128), f32), vm((32, 128), f32), vm((32, 128), f32),
            vm((ROWS, 128), f32), vm((ROWS, 128), f32), vm((ROWS, 128), f32),
            vm((ROWS, D), f32), vm((2, ROWS, D), bf), vm((ROWS, 512), bf), vm((ROWS, CHUNK), bf),
            vm((2, 8, 128), f32), vm((4, CHUNK, D), f32),
            vm((4, 4, 4, 4, 16, 128), bf), vm((4, 4, 4, 16, 128), bf), vm((4, 4, 16, 128), bf),
            vm((4, 3, 4, 4, 16, 128), bf), vm((4, 3, 4, 16, 128), bf), vm((4, 3, 16, 128), bf),
            vm((4, 8, 128), f32), vm((8, 128), f32), vm((3, 4, 8, 128), f32),
            sem((11,)), sem((3,)), sem((3,)), sem((4,)), sem((4,)),
            sem((2, 8)), sem((2, 8)), sem((4,)), sem((4,)), sem((4,)), sem((4,)),
            sem((4, 3)), sem((4, 3)), sem((4, 3)), sem((4, 3)), sem((4, 3)), sem((4, 3)),
            sem, sem, sem((3, 3)), sem((3, 3)),
        ],
        compiler_params=pltpu.CompilerParams(
            collective_id=0, has_side_effects=True, vmem_limit_bytes=44 << 20
        ),
        cost_estimate=pl.CostEstimate(
            flops=15 * 10**9, bytes_accessed=7 << 20, transcendentals=12 << 20
        ),
    )(*(
        pltpu.with_memory_space_constraint(value, pltpu.HBM)
        for value in (hidden, weight, stamps.reshape(8, 128), group_ids.reshape(8, 128))
    ))
    items = device_count * ROWS
    pair_count = items * (ROWS - 1) // 2 + 3 * items * ROWS // 2
    grad_hidden, grad_weight, loss = pl.pallas_call(
        functools.partial(scale_kernel, pair_count, items),
        out_shape=(
            jax.ShapeDtypeStruct((ROWS, FF), bf),
            jax.ShapeDtypeStruct((16, D), f32),
            jax.ShapeDtypeStruct((1, 1), f32),
        ),
        in_specs=[local, local, local],
        out_specs=(whole, local, local),
        scratch_shapes=[vm((ROWS, FF), bf), sem((8,))],
        compiler_params=pltpu.CompilerParams(vmem_limit_bytes=16 << 20),
        cost_estimate=pl.CostEstimate(
            flops=2 << 20, bytes_accessed=4 << 20, transcendentals=0
        ),
    )(grad, partial, totals)
    return grad_hidden, grad_weight, loss[0, 0]


def solution(mesh):
    in_specs = (P(("blk", "grp"), None), P(), P(("blk", "grp")), P(("blk", "grp")))
    out_specs = (P(("blk", "grp"), None), P(("blk", "grp"), None), P())
    return jax.shard_map(
        on_device, mesh=mesh, in_specs=in_specs, out_specs=out_specs, check_vma=False
    )
```

```python
import functools
import math

import jax
import jax.numpy as jnp
from jax import lax
from jax.experimental import pallas as pl
from jax.experimental.pallas import tpu as pltpu
from jax.sharding import PartitionSpec as P

ROWS = 1024
FF = 2048
D = 512
TAU = 64
CHUNK = 256
MESH = pl.DeviceIdType.MESH
NT = (((1,), (1,)), ((), ()))
TN = (((0,), (0,)), ((), ()))
SCALE2 = math.log2(math.e) / math.sqrt(D)
ORDERS = ("zxy", "yzx", "xyz", "mxn")


def place(x, y, z, c):
    return (x * 4 + (y % 2) * 2 + c, z * 2 + y // 2)


def kernel(
    hidden_hbm, weight_hbm, stamps_hbm, ids_hbm,
    gh_ref, gw_ref, tot_ref,
    hid, wgt, ht, htm, emb, aux, theirs, col_u, col_v, col_i, row_u, row_v, row_i,
    acc, summed, coef, coef_last, coef_end, sums, pown, part1, part2, part3, got1, got2, got3,
    tsend, tcore, taxis,
    in_sem, aux_send, aux_recv, core_send, core_recv, zx_send, zx_recv,
    f_send, f_recv, e_send, e_recv,
    h_send, h_recv, p_send, p_recv, s1_send, s1_recv, s2_send, s2_recv, s3_send, s3_recv,
    tc_send, tc_recv, ta_send, ta_recv,
):
    b = lax.axis_index("blk")
    g = lax.axis_index("grp")
    at = {"x": b // 4, "y": (g % 2) * 2 + (b // 2) % 2, "z": g // 2}
    core = b % 2

    at["m"] = at["z"] * (1 - core) + at["y"] * core
    at["n"] = at["y"] * (1 - core) + at["z"] * core

    def peer(axis, ahead):
        steps = {
            "x": (ahead, 0, 0), "y": (0, ahead, 0), "z": (0, 0, ahead),
            "m": (0, ahead * core, ahead * (1 - core)),
            "n": (0, ahead * (1 - core), ahead * core),
        }[axis]
        there = [(at[a] + step) % 4 for a, step in zip("xyz", steps)]
        return place(*there, core)

    core_mate = place(at["x"], at["y"], at["z"], 1 - core)
    partners = (core_mate, peer("z", 2), peer("x", 2))

    def remote(src, dst, send, recv, device):
        return pltpu.make_async_remote_copy(
            src_ref=src, dst_ref=dst, send_sem=send, recv_sem=recv,
            device_id=device, device_id_type=MESH,
        )

    def weight_in(i):
        lanes = pl.ds(i * 128, 128)
        return pltpu.make_async_copy(
            weight_hbm.at[:, lanes], wgt.at[:, lanes], in_sem.at[11 + i]
        )

    def hidden_in(i):
        rows = pl.ds(i * 128, 128)
        return pltpu.make_async_copy(hidden_hbm.at[rows], hid.at[rows], in_sem.at[i])

    def aux_in(k):
        return pltpu.make_async_copy((stamps_hbm, ids_hbm)[k], aux.at[k], in_sem.at[9 + k])

    def aux_copy(k):
        return remote(aux, theirs.at[k], aux_send.at[k], aux_recv.at[k], partners[k])

    def core_copy(i):
        return remote(
            emb.at[pl.ds(i * CHUNK, CHUNK)], emb.at[pl.ds(ROWS + i * CHUNK, CHUNK)],
            core_send.at[i], core_recv.at[i], core_mate,
        )

    def end_copy(n, k):
        return remote(
            emb.at[pl.ds(896 + n * 64, 64)],
            emb.at[pl.ds(4 * ROWS - CHUNK + n * 128 + k * 64, 64)],
            e_send.at[k, n], e_recv.at[k, n], partners[1 + k],
        )

    def zx_copy(i, k):
        return remote(
            emb.at[pl.ds(i * 128, 128)], emb.at[pl.ds(2 * ROWS + i * CHUNK + k * 128, 128)],
            zx_send.at[k, i], zx_recv.at[k, i], partners[1 + k],
        )

    def first_copy(n, k):
        lanes = pl.ds(n * 128, 128)
        return remote(
            emb.at[pl.ds(0, 128), lanes], emb.at[pl.ds(2 * ROWS + k * 128, 128), lanes],
            f_send.at[k, n], f_recv.at[k, n], partners[1 + k],
        )

    def h_copy(i):
        return remote(ht.at[1 - core, i], htm.at[i], h_send.at[i], h_recv.at[i], core_mate)

    def p_copy(i):
        rows = pl.ds(i * CHUNK, CHUNK)
        return remote(
            summed.at[0, rows], summed.at[1, rows], p_send.at[i], p_recv.at[i], core_mate
        )

    def stage_copy(p, stage, ahead):
        axis = ORDERS[p][stage]
        src, dst, send, recv = (
            (part1, got1, s1_send, s1_recv),
            (part2, got2, s2_send, s2_recv),
            (part3, got3, s3_send, s3_recv),
        )[stage]
        return remote(
            src.at[p, (at[axis] + ahead) % 4], dst.at[p, ahead - 1],
            send.at[p, ahead - 1], recv.at[p, ahead - 1], peer(axis, ahead),
        )

    def total_core():
        return remote(tsend.at[0], tcore, tc_send, tc_recv, core_mate)

    def total_axis(n, ahead):
        axis = "xyz"[n]
        return remote(
            tsend.at[1 + n], taxis.at[n, at[axis]],
            ta_send.at[n, ahead - 1], ta_recv.at[n, ahead - 1], peer(axis, ahead),
        )

    barrier = pltpu.get_barrier_semaphore()
    for device in partners[1:]:
        pl.semaphore_signal(barrier, inc=1, device_id=device, device_id_type=MESH)
    hidden_in(0).start()
    weight_in(0).start()
    pl.semaphore_signal(barrier, inc=1, device_id=core_mate, device_id_type=MESH)
    for axis in "zxy":
        for ahead in (1, 3) if axis != "y" else (2, 1, 3):
            pl.semaphore_signal(barrier, inc=1, device_id=peer(axis, ahead), device_id_type=MESH)
    for i in range(1, 4):
        weight_in(i).start()
    for k in range(2):
        aux_in(k).start()
    for i in range(1, 8):
        hidden_in(i).start()

    def embed(first, count):
        for n in range(count // 128):
            hidden_in(first // 128 + n).wait()
        rows = pl.ds(first, count)
        emb[rows, :] = jnp.dot(
            hid[rows, :], wgt[...], preferred_element_type=jnp.float32
        ).astype(jnp.bfloat16)

    hidden_in(0).wait()
    for n in range(4):
        lanes = slice(n * 128, (n + 1) * 128)
        weight_in(n).wait()
        emb[:128, lanes] = jnp.dot(
            hid[:128, :], wgt[:, lanes], preferred_element_type=jnp.float32
        ).astype(jnp.bfloat16)
        if n == 0:
            pl.semaphore_wait(barrier, 10)
        for k in range(2):
            first_copy(n, k).start()
    for k in range(2):
        aux_in(k).wait()
    for k in range(3):
        aux_copy(k).start()
    embed(128, 128)
    for k in range(2):
        zx_copy(1, k).start()
    core_copy(0).start()

    def embed_rest(i, carry):
        embed(pl.multiple_of(i * CHUNK, CHUNK), CHUNK)
        for h in range(2):
            for k in range(2):
                zx_copy(2 * i + h, k).start()
        core_copy(i).start()
        return carry

    lax.fori_loop(1, 3, embed_rest, 0)
    embed(768, CHUNK)
    for k in range(2):
        zx_copy(6, k).start()
    for n in range(2):
        for k in range(2):
            end_copy(n, k).start()
    core_copy(3).start()

    def columns(place_of, stamps, ids):
        times = stamps.astype(jnp.float32) * (1.0 / TAU)
        values = (jnp.exp(times), jnp.exp(-times), ids.astype(jnp.float32))
        for value, ref in zip(values, (col_u, col_v, col_i)):
            for r in range(8):
                ref[place_of(r) : place_of(r) + 1, :] = value[r : r + 1, :]
        return values

    u, v, names = columns(lambda r: r, aux[0], aux[1])
    ln2 = math.log(2.0)
    stack = jnp.concatenate(
        [u * ln2, v * ln2, names, jnp.zeros((104, 128), jnp.float32)], axis=0
    ).T
    for k, rows in enumerate((row_u, row_v, row_i)):
        for r in range(8):
            column = stack[:, k * 8 + r : k * 8 + r + 1]
            rows[r * 128 : (r + 1) * 128, :] = jnp.broadcast_to(column, (128, 128))
    acc[...] = jnp.zeros_like(acc)
    sums[...] = jnp.zeros_like(sums)

    def sweep(tiles, width, coef, last=False):
        sides = {}
        for _, first, _, _ in tiles:
            if id(first) not in sides:
                sides[id(first)] = (
                    emb[pl.ds(pl.multiple_of(first, width), width), :],
                    [
                        [ref[pl.ds(first // 128 + h, 1), :] for ref in (col_u, col_v, col_i)]
                        for h in range(width // 128)
                    ],
                )
        loss = [jnp.zeros((8, 128), jnp.float32), jnp.zeros((8, 128), jnp.float32)]
        total = [jnp.zeros((8, 128), jnp.float32), jnp.zeros((8, 128), jnp.float32)]

        def scores(tile):
            r, first = tile[:2]
            return lax.dot_general(
                emb[r * CHUNK : (r + 1) * CHUNK, :], sides[id(first)][0], NT,
                preferred_element_type=jnp.float32,
            )

        def gather(t):
            r, first, _, mirror = tiles[t]
            rows = slice(r * CHUNK, (r + 1) * CHUNK)
            held = coef[t % 4 * CHUNK : (t % 4 + 1) * CHUNK, :]
            v = acc[rows, :] + jnp.dot(
                held, sides[id(first)][0], preferred_element_type=jnp.float32
            )
            if last:
                summed[0, rows, :] = v.astype(jnp.bfloat16)
                p_copy(r).start()
                if r == 1:
                    own_half(0)
            else:
                acc[rows, :] = v
            if mirror:
                there = slice(first, first + width)
                acc[there, :] += lax.dot_general(
                    held, emb[rows, :], TN, preferred_element_type=jnp.float32
                )

        s = scores(tiles[0])
        for t, (r, first, diagonal, mirror) in enumerate(tiles):
            s_next = scores(tiles[t + 1]) if t + 1 < len(tiles) else None
            if t > 0:
                gather(t - 1)
            cols = sides[id(first)][1]
            for q in range(8):
                lo = r * CHUNK + q * 32
                at_coef = t % 4 * CHUNK + q * 32
                ru, rv, ri = row_u[lo : lo + 32, :], row_v[lo : lo + 32, :], row_i[lo : lo + 32, :]
                for h in range(width // 128):
                    cu, cv, ci = cols[h]
                    sign = jnp.where(ri == ci, -SCALE2, SCALE2)
                    m = s[q * 32 : (q + 1) * 32, h * 128 : (h + 1) * 128] * sign
                    plus = jnp.maximum(m, jnp.log2(1.0 + jnp.exp2(jnp.minimum(m, 100.0))))
                    w = jnp.minimum(ru * cv, rv * cu)
                    if diagonal and lo // 128 == first // 128 + h:
                        i = lax.broadcasted_iota(jnp.int32, (32, 128), 0) + lo % 128
                        j = lax.broadcasted_iota(jnp.int32, (32, 128), 1)
                        w = jnp.where(i == j, 0.0, w)
                    c = (w * sign) * jnp.exp2(m - plus)
                    coef[at_coef : at_coef + 32, h * 128 : (h + 1) * 128] = c.astype(jnp.bfloat16)
                    term = w * plus
                    for n in range(4):
                        loss[mirror] = loss[mirror] + term[n * 8 : (n + 1) * 8]
                        total[mirror] = total[mirror] + w[n * 8 : (n + 1) * 8]
            s = s_next
        gather(len(tiles) - 1)
        sums[0] += total[0] + 2.0 * total[1]
        sums[1] += loss[0] + 2.0 * loss[1]

    def own_half(k):
        depth = slice(k * 512, (k + 1) * 512)
        for x in range(4):
            block = ht[core, x, :, :, :, depth].reshape(CHUNK, 512)
            v = jnp.dot(block, summed[0, depth, :], preferred_element_type=jnp.float32)
            if k:
                v = v + pown[x]
            pown[x] = v

    low, high = 0, 512
    sweep(
        [(0, low, True, False), (1, low, True, False), (0, high, False, True),
         (1, high, False, True), (2, high, True, False), (3, high, True, False)],
        512, coef,
    )

    for k in range(3):
        aux_copy(k).wait_recv()
    columns(lambda r: 8 + r, theirs[0, 0], theirs[0, 1])
    columns(lambda r: 16 + 2 * r, theirs[1, 0], theirs[1, 1])
    columns(lambda r: 17 + 2 * r, theirs[2, 0], theirs[2, 1])
    for ref in (col_u, col_v, col_i):
        z_row, x_row = ref[30:31, :], ref[31:32, :]
        ref[30:31, :] = jnp.concatenate([z_row[:, :64], x_row[:, :64]], axis=1)
        ref[31:32, :] = jnp.concatenate([z_row[:, 64:], x_row[:, 64:]], axis=1)

    def turn(x, carry):
        for n in range(4):
            lanes = pl.ds(pl.multiple_of(x * 512 + n * 128, 128), 128)
            turned = hid[:, lanes].T
            for k in range(8):
                ht[n % 2, x, (k % 2) * 2 + n // 2, k // 2] = turned[k * 16 : (k + 1) * 16, :]
        h_copy(x).start()
        return carry

    def other_step(i, carry):
        @pl.when(i < 2)
        def _():
            for n in range(2):
                core_copy(2 * i + n).wait_recv()

        @pl.when(i == 2)
        def _():
            lax.fori_loop(0, 4, turn, 0)

        @pl.when(i == 2)
        def _():
            for k in range(2):
                for n in range(4):
                    first_copy(n, k).wait_recv()

        @pl.when(i > 2)
        def _():
            for k in range(2):
                zx_copy(2 * (i - 2), k).wait_recv()

        @pl.when(i >= 2)
        def _():
            for k in range(2):
                zx_copy(2 * (i - 2) + 1, k).wait_recv()

        first = ROWS + i * 512
        sweep([(r, first, False, False) for r in range(4)], 512, coef)
        return carry

    lax.fori_loop(0, 5, other_step, 0)

    for k in range(2):
        zx_copy(6, k).wait_recv()
    first = 4 * ROWS - 2 * CHUNK
    sweep([(r, first, False, False) for r in range(4)], CHUNK, coef_last)
    for n in range(2):
        for k in range(2):
            end_copy(n, k).wait_recv()
        first = 4 * ROWS - CHUNK + n * 128
        sweep([(r, first, False, False) for r in range(4)], 128, coef_end, last=n == 1)

    line = lax.broadcasted_iota(jnp.int32, (8, 128), 0)
    w_sum = jnp.sum(sums[0], axis=0, keepdims=True)
    l_sum = jnp.sum(sums[1], axis=0, keepdims=True)
    tsend[0] = jnp.where(line == 0, w_sum, jnp.where(line == 1, l_sum, 0.0))
    total_core().start()

    own_half(1)
    for i in range(4):
        h_copy(i).wait_recv()

    def mate_part(x, lanes, k):
        depth = slice(k * 512, (k + 1) * 512)
        return pown[x, :, lanes] + jnp.dot(
            htm[x, :, :, :, depth].reshape(CHUNK, 512), summed[1, depth, lanes],
            preferred_element_type=jnp.float32,
        )

    for i in range(2):
        p_copy(i).wait_recv()
    for x in range(4):
        pown[x] = mate_part(x, slice(0, D), 0)
    for i in range(2, 4):
        p_copy(i).wait_recv()

    def mate_half(pair):
        for x in range(4):
            v = mate_part(x, slice(pair * 256, (pair + 1) * 256), 1)
            v = v.astype(jnp.bfloat16).reshape(4, 4, 16, 256)
            if pair == 0:
                for y in range(4):
                    part1[0, :, x, y] = v[y, :, :, :128]
                part1[1, :, :, x] = v[..., 128:]
            else:
                part1[2, x] = v[..., :128]
                for y in range(4):
                    for z in range(4):
                        m = z * (1 - core) + y * core
                        n = y * (1 - core) + z * core
                        part1[3, m, x, n] = v[y, z, :, 128:]
        for p in (2 * pair, 2 * pair + 1):
            for ahead in (2, 1, 3):
                stage_copy(p, 0, ahead).start()

    mate_half(0)
    mate_half(1)
    total_core().wait_recv()

    def spread(n, value):
        tsend[1 + n] = value
        taxis[n, at["xyz"[n]]] = value
        for ahead in (2, 1, 3):
            total_axis(n, ahead).start()

    def gathered(n):
        for ahead in (1, 2, 3):
            total_axis(n, ahead).wait_recv()
        return (taxis[n, 0] + taxis[n, 1]) + (taxis[n, 2] + taxis[n, 3])

    spread(0, tsend[0] + tcore[...])

    def grad_rows(i, carry):
        rows = pl.ds(pl.multiple_of(i * CHUNK, CHUNK), CHUNK)
        for n in range(4):
            gh_ref[rows, n * 512 : (n + 1) * 512] = lax.dot_general(
                summed[0, rows, :], wgt[n * 512 : (n + 1) * 512, :], NT,
                preferred_element_type=jnp.float32,
            ).astype(jnp.bfloat16)
        return carry

    lax.fori_loop(0, 4, grad_rows, 0)

    for k in range(3):
        aux_copy(k).wait_send()
    for i in range(4):
        core_copy(i).wait_send()
        h_copy(i).wait_send()
        p_copy(i).wait_send()
    for k in range(2):
        for n in range(4):
            first_copy(n, k).wait_send()
        for n in range(2):
            end_copy(n, k).wait_send()
        for i in range(1, 7):
            zx_copy(i, k).wait_send()
    total_core().wait_send()

    def sent(stage):
        for ahead in (1, 2, 3):
            for p in range(4):
                stage_copy(p, stage, ahead).wait_send()
            total_axis(stage, ahead).wait_send()

    def reduced(p, stage):
        src, got = ((part1, got1), (part2, got2), (part3, got3))[stage]
        for ahead in (1, 2, 3):
            stage_copy(p, stage, ahead).wait_recv()
        v = src[p, at[ORDERS[p][stage]]].astype(jnp.float32)
        for n in range(3):
            v = v + got[p, n].astype(jnp.float32)
        return v

    for p in range(4):
        part2[p] = reduced(p, 0).astype(jnp.bfloat16)
        for ahead in (2, 1, 3):
            stage_copy(p, 1, ahead).start()
    spread(1, gathered(0))
    sent(0)

    for p in range(4):
        part3[p] = reduced(p, 1).astype(jnp.bfloat16)
        for ahead in (2, 1, 3):
            stage_copy(p, 2, ahead).start()
    spread(2, gathered(1))
    sent(1)

    for p in range(4):
        gw_ref[:, p * 128 : (p + 1) * 128] = reduced(p, 2)
    tot_ref[...] = jnp.broadcast_to(
        jnp.sum(gathered(2), axis=1, keepdims=True), (8, 128)
    )

    for ahead in (1, 2, 3):
        for p in range(4):
            stage_copy(p, 2, ahead).wait_send()
        total_axis(2, ahead).wait_send()


def scale_kernel(
    pair_count, items, gh_ref, gw_ref, tot_ref, gh_out, gw_out, loss_out, buf, gw_buf, loss_buf, sem
):
    totals = tot_ref[...]
    weight_total = totals[0:1, :] * (0.5 / math.log(2.0))
    pair_loss = totals[1:2, :] * 0.5
    inverse = float(pair_count) / weight_total
    across = jnp.broadcast_to(jnp.concatenate([inverse] * 16, axis=1), (16, FF))
    gw_buf[...] = gw_ref[...] * (across[:, :D] * (1.0 / items))
    loss_buf[...] = (pair_loss / weight_total)[:, 0:1]
    small = (
        pltpu.make_async_copy(gw_buf, gw_out, sem.at[8]),
        pltpu.make_async_copy(loss_buf, loss_out, sem.at[9]),
    )
    for copy in small:
        copy.start()

    def out(i):
        rows = pl.ds(i * 128, 128)
        return pltpu.make_async_copy(buf.at[rows], gh_out.at[rows], sem.at[i])

    for i in range(8):
        for n in range(8):
            rows = slice(i * 128 + n * 16, i * 128 + (n + 1) * 16)
            buf[rows, :] = (gh_ref[rows, :].astype(jnp.float32) * across).astype(jnp.bfloat16)
        out(i).start()
    for i in range(8):
        out(i).wait()
    for copy in small:
        copy.wait()


def on_device(hidden, weight, stamps, group_ids):
    device_count = lax.axis_size("blk") * lax.axis_size("grp")
    bf, f32 = jnp.bfloat16, jnp.float32
    sem = pltpu.SemaphoreType.DMA
    vm = pltpu.VMEM
    whole = pl.BlockSpec(memory_space=pl.ANY)
    outside = pl.BlockSpec(memory_space=pltpu.HBM)
    local = pl.BlockSpec(memory_space=pltpu.VMEM)
    grad, partial, totals = pl.pallas_call(
        kernel,
        out_shape=(
            pltpu.VMEM((ROWS, FF), bf),
            pltpu.VMEM((16, D), f32),
            pltpu.VMEM((8, 128), f32),
        ),
        in_specs=[outside] * 4,
        out_specs=(local, local, local),
        scratch_shapes=[
            vm((ROWS, FF), bf), vm((FF, D), bf), vm((2, 4, 4, 4, 16, ROWS), bf),
            vm((4, 4, 4, 16, ROWS), bf), vm((4 * ROWS, D), bf),
            vm((2, 8, 128), jnp.int32), vm((3, 2, 8, 128), jnp.int32),
            vm((32, 128), f32), vm((32, 128), f32), vm((32, 128), f32),
            vm((ROWS, 128), f32), vm((ROWS, 128), f32), vm((ROWS, 128), f32),
            vm((ROWS, D), f32), vm((2, ROWS, D), bf), vm((ROWS, 512), bf), vm((ROWS, CHUNK), bf), vm((ROWS, 128), bf),
            vm((2, 8, 128), f32), vm((4, CHUNK, D), f32),
            vm((4, 4, 4, 4, 16, 128), bf), vm((4, 4, 4, 16, 128), bf), vm((4, 4, 16, 128), bf),
            vm((4, 3, 4, 4, 16, 128), bf), vm((4, 3, 4, 16, 128), bf), vm((4, 3, 16, 128), bf),
            vm((4, 8, 128), f32), vm((8, 128), f32), vm((3, 4, 8, 128), f32),
            sem((15,)), sem((3,)), sem((3,)), sem((4,)), sem((4,)),
            sem((2, 8)), sem((2, 8)), sem((2, 4)), sem((2, 4)), sem((2, 2)), sem((2, 2)), sem((4,)), sem((4,)), sem((4,)), sem((4,)),
            sem((4, 3)), sem((4, 3)), sem((4, 3)), sem((4, 3)), sem((4, 3)), sem((4, 3)),
            sem, sem, sem((3, 3)), sem((3, 3)),
        ],
        compiler_params=pltpu.CompilerParams(
            collective_id=0, has_side_effects=True, vmem_limit_bytes=44 << 20
        ),
        cost_estimate=pl.CostEstimate(
            flops=15 * 10**9, bytes_accessed=7 << 20, transcendentals=12 << 20
        ),
    )(*(
        pltpu.with_memory_space_constraint(value, pltpu.HBM)
        for value in (hidden, weight, stamps.reshape(8, 128), group_ids.reshape(8, 128))
    ))
    items = device_count * ROWS
    pair_count = items * (ROWS - 1) // 2 + 3 * items * ROWS // 2
    grad_hidden, grad_weight, loss = pl.pallas_call(
        functools.partial(scale_kernel, pair_count, items),
        out_shape=(
            jax.ShapeDtypeStruct((ROWS, FF), bf),
            jax.ShapeDtypeStruct((16, D), f32),
            jax.ShapeDtypeStruct((1, 1), f32),
        ),
        in_specs=[local, local, local],
        out_specs=(whole, whole, whole),
        scratch_shapes=[vm((ROWS, FF), bf), vm((16, D), f32), vm((1, 1), f32), sem((10,))],
        compiler_params=pltpu.CompilerParams(vmem_limit_bytes=16 << 20),
        cost_estimate=pl.CostEstimate(
            flops=2 << 20, bytes_accessed=4 << 20, transcendentals=0
        ),
    )(grad, partial, totals)
    return grad_hidden, grad_weight, loss[0, 0]


def solution(mesh):
    in_specs = (P(("blk", "grp"), None), P(), P(("blk", "grp")), P(("blk", "grp")))
    out_specs = (P(("blk", "grp"), None), P(("blk", "grp"), None), P())
    return jax.shard_map(
        on_device, mesh=mesh, in_specs=in_specs, out_specs=out_specs, check_vma=False
    )
```

```python
import functools
import math

import jax
import jax.numpy as jnp
from jax import lax
from jax.experimental import pallas as pl
from jax.experimental.pallas import tpu as pltpu
from jax.sharding import PartitionSpec as P

ROWS = 1024
FF = 2048
D = 512
TAU = 64
CHUNK = 256
MESH = pl.DeviceIdType.MESH
NT = (((1,), (1,)), ((), ()))
TN = (((0,), (0,)), ((), ()))
SMALL = 2.0**-12
SCALE2 = math.log2(math.e) / math.sqrt(D)
ORDERS = ("zxy", "yzx", "xyz", "mxn")


def place(x, y, z, c):
    return (x * 4 + (y % 2) * 2 + c, z * 2 + y // 2)


def kernel(
    hidden_hbm, weight_hbm, stamps_hbm, ids_hbm,
    gh_ref, gw_ref, tot_ref,
    hid, wgt, ht, htm, emb, aux, theirs, col_u, col_v, col_i, row_u, row_v, row_i,
    acc, summed, coef, coef_last, coef_end, sums, pown, part1, part2, part3, got1, got2, got3,
    tsend, tcore, taxis,
    in_sem, aux_send, aux_recv, core_send, core_recv, zx_send, zx_recv,
    f_send, f_recv, e_send, e_recv,
    h_send, h_recv, p_send, p_recv, s1_send, s1_recv, s2_send, s2_recv, s3_send, s3_recv,
    tc_send, tc_recv, ta_send, ta_recv,
):
    b = lax.axis_index("blk")
    g = lax.axis_index("grp")
    at = {"x": b // 4, "y": (g % 2) * 2 + (b // 2) % 2, "z": g // 2}
    core = b % 2

    at["m"] = at["z"] * (1 - core) + at["y"] * core
    at["n"] = at["y"] * (1 - core) + at["z"] * core

    def peer(axis, ahead):
        steps = {
            "x": (ahead, 0, 0), "y": (0, ahead, 0), "z": (0, 0, ahead),
            "m": (0, ahead * core, ahead * (1 - core)),
            "n": (0, ahead * (1 - core), ahead * core),
        }[axis]
        there = [(at[a] + step) % 4 for a, step in zip("xyz", steps)]
        return place(*there, core)

    core_mate = place(at["x"], at["y"], at["z"], 1 - core)
    partners = (core_mate, peer("z", 2), peer("x", 2))

    def remote(src, dst, send, recv, device):
        return pltpu.make_async_remote_copy(
            src_ref=src, dst_ref=dst, send_sem=send, recv_sem=recv,
            device_id=device, device_id_type=MESH,
        )

    def weight_in(i):
        lanes = pl.ds(i * 128, 128)
        return pltpu.make_async_copy(
            weight_hbm.at[:, lanes], wgt.at[:, lanes], in_sem.at[11 + i]
        )

    def hidden_in(i):
        rows = pl.ds(i * 128, 128)
        return pltpu.make_async_copy(hidden_hbm.at[rows], hid.at[rows], in_sem.at[i])

    def aux_in(k):
        return pltpu.make_async_copy((stamps_hbm, ids_hbm)[k], aux.at[k], in_sem.at[9 + k])

    def aux_copy(k):
        return remote(aux, theirs.at[k], aux_send.at[k], aux_recv.at[k], partners[k])

    def core_copy(i):
        return remote(
            emb.at[pl.ds(i * CHUNK, CHUNK)], emb.at[pl.ds(ROWS + i * CHUNK, CHUNK)],
            core_send.at[i], core_recv.at[i], core_mate,
        )

    def end_copy(n, k):
        return remote(
            emb.at[pl.ds(896 + n * 64, 64)],
            emb.at[pl.ds(4 * ROWS - CHUNK + n * 128 + k * 64, 64)],
            e_send.at[k, n], e_recv.at[k, n], partners[1 + k],
        )

    def zx_copy(i, k):
        return remote(
            emb.at[pl.ds(i * 128, 128)], emb.at[pl.ds(2 * ROWS + i * CHUNK + k * 128, 128)],
            zx_send.at[k, i], zx_recv.at[k, i], partners[1 + k],
        )

    def first_copy(n, k):
        lanes = pl.ds(n * 128, 128)
        return remote(
            emb.at[pl.ds(0, 128), lanes], emb.at[pl.ds(2 * ROWS + k * 128, 128), lanes],
            f_send.at[k, n], f_recv.at[k, n], partners[1 + k],
        )

    def h_copy(i):
        return remote(ht.at[1 - core, i], htm.at[i], h_send.at[i], h_recv.at[i], core_mate)

    def p_copy(i):
        rows = pl.ds(i * CHUNK, CHUNK)
        return remote(
            summed.at[0, rows], summed.at[1, rows], p_send.at[i], p_recv.at[i], core_mate
        )

    def stage_copy(p, stage, ahead):
        axis = ORDERS[p][stage]
        src, dst, send, recv = (
            (part1, got1, s1_send, s1_recv),
            (part2, got2, s2_send, s2_recv),
            (part3, got3, s3_send, s3_recv),
        )[stage]
        return remote(
            src.at[p, (at[axis] + ahead) % 4], dst.at[p, ahead - 1],
            send.at[p, ahead - 1], recv.at[p, ahead - 1], peer(axis, ahead),
        )

    def total_core():
        return remote(tsend.at[0], tcore, tc_send, tc_recv, core_mate)

    def total_axis(n, ahead):
        axis = "xyz"[n]
        return remote(
            tsend.at[1 + n], taxis.at[n, at[axis]],
            ta_send.at[n, ahead - 1], ta_recv.at[n, ahead - 1], peer(axis, ahead),
        )

    barrier = pltpu.get_barrier_semaphore()
    for device in partners[1:]:
        pl.semaphore_signal(barrier, inc=1, device_id=device, device_id_type=MESH)
    hidden_in(0).start()
    weight_in(0).start()
    pl.semaphore_signal(barrier, inc=1, device_id=core_mate, device_id_type=MESH)
    for axis in "zxy":
        for ahead in (1, 3) if axis != "y" else (2, 1, 3):
            pl.semaphore_signal(barrier, inc=1, device_id=peer(axis, ahead), device_id_type=MESH)
    for i in range(1, 4):
        weight_in(i).start()
    for k in range(2):
        aux_in(k).start()
    for i in range(1, 8):
        hidden_in(i).start()

    def embed(first, count):
        for n in range(count // 128):
            hidden_in(first // 128 + n).wait()
        rows = pl.ds(first, count)
        emb[rows, :] = jnp.dot(
            hid[rows, :], wgt[...], preferred_element_type=jnp.float32
        ).astype(jnp.bfloat16)

    hidden_in(0).wait()
    for n in range(4):
        lanes = slice(n * 128, (n + 1) * 128)
        weight_in(n).wait()
        emb[:128, lanes] = jnp.dot(
            hid[:128, :], wgt[:, lanes], preferred_element_type=jnp.float32
        ).astype(jnp.bfloat16)
        if n == 0:
            pl.semaphore_wait(barrier, 10)
        for k in range(2):
            first_copy(n, k).start()
    for k in range(2):
        aux_in(k).wait()
    for k in range(3):
        aux_copy(k).start()
    embed(128, 128)
    for k in range(2):
        zx_copy(1, k).start()
    core_copy(0).start()

    def embed_rest(i, carry):
        embed(pl.multiple_of(i * CHUNK, CHUNK), CHUNK)
        for h in range(2):
            for k in range(2):
                zx_copy(2 * i + h, k).start()
        core_copy(i).start()
        return carry

    lax.fori_loop(1, 3, embed_rest, 0)
    embed(768, CHUNK)
    for k in range(2):
        zx_copy(6, k).start()
    for n in range(2):
        for k in range(2):
            end_copy(n, k).start()
    core_copy(3).start()

    def columns(place_of, stamps, ids):
        times = stamps.astype(jnp.float32) * (1.0 / TAU)
        values = (jnp.exp(times), jnp.exp(-times), ids.astype(jnp.float32))
        for value, ref in zip(values, (col_u, col_v, col_i)):
            for r in range(8):
                ref[place_of(r) : place_of(r) + 1, :] = value[r : r + 1, :]
        return values

    u, v, names = columns(lambda r: r, aux[0], aux[1])
    ln2 = math.log(2.0)
    stack = jnp.concatenate(
        [u * ln2, v * ln2, names, jnp.zeros((104, 128), jnp.float32)], axis=0
    ).T
    for k, rows in enumerate((row_u, row_v, row_i)):
        for r in range(8):
            column = stack[:, k * 8 + r : k * 8 + r + 1]
            rows[r * 128 : (r + 1) * 128, :] = jnp.broadcast_to(column, (128, 128))
    acc[...] = jnp.zeros_like(acc)
    sums[...] = jnp.zeros_like(sums)

    def sweep(tiles, width, coef, last=False):
        sides = {}
        for _, first, _, _ in tiles:
            if id(first) not in sides:
                sides[id(first)] = (
                    emb[pl.ds(pl.multiple_of(first, width), width), :],
                    [
                        [ref[pl.ds(first // 128 + h, 1), :] for ref in (col_u, col_v, col_i)]
                        for h in range(width // 128)
                    ],
                )
        loss = [jnp.zeros((8, 128), jnp.float32), jnp.zeros((8, 128), jnp.float32)]
        total = [jnp.zeros((8, 128), jnp.float32), jnp.zeros((8, 128), jnp.float32)]

        def scores(tile):
            r, first = tile[:2]
            return lax.dot_general(
                emb[r * CHUNK : (r + 1) * CHUNK, :], sides[id(first)][0], NT,
                preferred_element_type=jnp.float32,
            )

        def gather(t):
            r, first, _, mirror = tiles[t]
            rows = slice(r * CHUNK, (r + 1) * CHUNK)
            held = coef[t % 4 * CHUNK : (t % 4 + 1) * CHUNK, :]
            v = acc[rows, :] + jnp.dot(
                held, sides[id(first)][0], preferred_element_type=jnp.float32
            )
            if last:
                summed[0, rows, :] = v.astype(jnp.bfloat16)
                p_copy(r).start()
                if r == 1:
                    own_half(0)
            else:
                acc[rows, :] = v
            if mirror:
                there = slice(first, first + width)
                acc[there, :] += lax.dot_general(
                    held, emb[rows, :], TN, preferred_element_type=jnp.float32
                )

        s = scores(tiles[0])
        for t, (r, first, diagonal, mirror) in enumerate(tiles):
            s_next = scores(tiles[t + 1]) if t + 1 < len(tiles) else None
            if t > 0:
                gather(t - 1)
            cols = sides[id(first)][1]
            for q in range(8):
                lo = r * CHUNK + q * 32
                at_coef = t % 4 * CHUNK + q * 32
                ru, rv, ri = row_u[lo : lo + 32, :], row_v[lo : lo + 32, :], row_i[lo : lo + 32, :]
                for h in range(width // 128):
                    cu, cv, ci = cols[h]
                    sign = jnp.where(ri == ci, -SCALE2, SCALE2)
                    m = s[q * 32 : (q + 1) * 32, h * 128 : (h + 1) * 128] * sign
                    e = jnp.exp2(jnp.minimum(m, 100.0))
                    near = jnp.where(e < SMALL, e * math.log2(math.e), jnp.log2(1.0 + e))
                    plus = jnp.maximum(m, near)
                    w = jnp.minimum(ru * cv, rv * cu)
                    if diagonal and lo // 128 == first // 128 + h:
                        i = lax.broadcasted_iota(jnp.int32, (32, 128), 0) + lo % 128
                        j = lax.broadcasted_iota(jnp.int32, (32, 128), 1)
                        w = jnp.where(i == j, 0.0, w)
                    c = (w * sign) * jnp.exp2(m - plus)
                    coef[at_coef : at_coef + 32, h * 128 : (h + 1) * 128] = c.astype(jnp.bfloat16)
                    term = w * plus
                    for n in range(4):
                        loss[mirror] = loss[mirror] + term[n * 8 : (n + 1) * 8]
                        total[mirror] = total[mirror] + w[n * 8 : (n + 1) * 8]
            s = s_next
        gather(len(tiles) - 1)
        sums[0] += total[0] + 2.0 * total[1]
        sums[1] += loss[0] + 2.0 * loss[1]

    def own_half(k):
        depth = slice(k * 512, (k + 1) * 512)
        for x in range(4):
            block = ht[core, x, :, :, :, depth].reshape(CHUNK, 512)
            v = jnp.dot(block, summed[0, depth, :], preferred_element_type=jnp.float32)
            if k:
                v = v + pown[x]
            pown[x] = v

    low, high = 0, 512
    sweep(
        [(0, low, True, False), (1, low, True, False), (0, high, False, True),
         (1, high, False, True), (2, high, True, False), (3, high, True, False)],
        512, coef,
    )

    for k in range(3):
        aux_copy(k).wait_recv()
    columns(lambda r: 8 + r, theirs[0, 0], theirs[0, 1])
    columns(lambda r: 16 + 2 * r, theirs[1, 0], theirs[1, 1])
    columns(lambda r: 17 + 2 * r, theirs[2, 0], theirs[2, 1])
    for ref in (col_u, col_v, col_i):
        z_row, x_row = ref[30:31, :], ref[31:32, :]
        ref[30:31, :] = jnp.concatenate([z_row[:, :64], x_row[:, :64]], axis=1)
        ref[31:32, :] = jnp.concatenate([z_row[:, 64:], x_row[:, 64:]], axis=1)

    def turn(x, carry):
        for n in range(4):
            lanes = pl.ds(pl.multiple_of(x * 512 + n * 128, 128), 128)
            turned = hid[:, lanes].T
            for k in range(8):
                ht[n % 2, x, (k % 2) * 2 + n // 2, k // 2] = turned[k * 16 : (k + 1) * 16, :]
        h_copy(x).start()
        return carry

    def other_step(i, carry):
        @pl.when(i < 2)
        def _():
            for n in range(2):
                core_copy(2 * i + n).wait_recv()

        @pl.when(i == 2)
        def _():
            lax.fori_loop(0, 4, turn, 0)

        @pl.when(i == 2)
        def _():
            for k in range(2):
                for n in range(4):
                    first_copy(n, k).wait_recv()

        @pl.when(i > 2)
        def _():
            for k in range(2):
                zx_copy(2 * (i - 2), k).wait_recv()

        @pl.when(i >= 2)
        def _():
            for k in range(2):
                zx_copy(2 * (i - 2) + 1, k).wait_recv()

        first = ROWS + i * 512
        sweep([(r, first, False, False) for r in range(4)], 512, coef)
        return carry

    lax.fori_loop(0, 5, other_step, 0)

    for k in range(2):
        zx_copy(6, k).wait_recv()
    first = 4 * ROWS - 2 * CHUNK
    sweep([(r, first, False, False) for r in range(4)], CHUNK, coef_last)
    for n in range(2):
        for k in range(2):
            end_copy(n, k).wait_recv()
        first = 4 * ROWS - CHUNK + n * 128
        sweep([(r, first, False, False) for r in range(4)], 128, coef_end, last=n == 1)

    line = lax.broadcasted_iota(jnp.int32, (8, 128), 0)
    w_sum = jnp.sum(sums[0], axis=0, keepdims=True)
    l_sum = jnp.sum(sums[1], axis=0, keepdims=True)
    tsend[0] = jnp.where(line == 0, w_sum, jnp.where(line == 1, l_sum, 0.0))
    total_core().start()

    own_half(1)
    for i in range(4):
        h_copy(i).wait_recv()

    def mate_part(x, lanes, k):
        depth = slice(k * 512, (k + 1) * 512)
        return pown[x, :, lanes] + jnp.dot(
            htm[x, :, :, :, depth].reshape(CHUNK, 512), summed[1, depth, lanes],
            preferred_element_type=jnp.float32,
        )

    for i in range(2):
        p_copy(i).wait_recv()
    for x in range(4):
        pown[x] = mate_part(x, slice(0, D), 0)
    for i in range(2, 4):
        p_copy(i).wait_recv()

    def mate_half(pair):
        for x in range(4):
            v = mate_part(x, slice(pair * 256, (pair + 1) * 256), 1)
            v = v.astype(jnp.bfloat16).reshape(4, 4, 16, 256)
            if pair == 0:
                for y in range(4):
                    part1[0, :, x, y] = v[y, :, :, :128]
                part1[1, :, :, x] = v[..., 128:]
            else:
                part1[2, x] = v[..., :128]
                for y in range(4):
                    for z in range(4):
                        m = z * (1 - core) + y * core
                        n = y * (1 - core) + z * core
                        part1[3, m, x, n] = v[y, z, :, 128:]
        for p in (2 * pair, 2 * pair + 1):
            for ahead in (2, 1, 3):
                stage_copy(p, 0, ahead).start()

    mate_half(0)
    mate_half(1)
    total_core().wait_recv()

    def spread(n, value):
        tsend[1 + n] = value
        taxis[n, at["xyz"[n]]] = value
        for ahead in (2, 1, 3):
            total_axis(n, ahead).start()

    def gathered(n):
        for ahead in (1, 2, 3):
            total_axis(n, ahead).wait_recv()
        return (taxis[n, 0] + taxis[n, 1]) + (taxis[n, 2] + taxis[n, 3])

    spread(0, tsend[0] + tcore[...])

    def grad_rows(i, carry):
        rows = pl.ds(pl.multiple_of(i * CHUNK, CHUNK), CHUNK)
        for n in range(4):
            gh_ref[rows, n * 512 : (n + 1) * 512] = lax.dot_general(
                summed[0, rows, :], wgt[n * 512 : (n + 1) * 512, :], NT,
                preferred_element_type=jnp.float32,
            ).astype(jnp.bfloat16)
        return carry

    lax.fori_loop(0, 4, grad_rows, 0)

    for k in range(3):
        aux_copy(k).wait_send()
    for i in range(4):
        core_copy(i).wait_send()
        h_copy(i).wait_send()
        p_copy(i).wait_send()
    for k in range(2):
        for n in range(4):
            first_copy(n, k).wait_send()
        for n in range(2):
            end_copy(n, k).wait_send()
        for i in range(1, 7):
            zx_copy(i, k).wait_send()
    total_core().wait_send()

    def sent(stage):
        for ahead in (1, 2, 3):
            for p in range(4):
                stage_copy(p, stage, ahead).wait_send()
            total_axis(stage, ahead).wait_send()

    def reduced(p, stage):
        src, got = ((part1, got1), (part2, got2), (part3, got3))[stage]
        for ahead in (1, 2, 3):
            stage_copy(p, stage, ahead).wait_recv()
        v = src[p, at[ORDERS[p][stage]]].astype(jnp.float32)
        for n in range(3):
            v = v + got[p, n].astype(jnp.float32)
        return v

    for p in range(4):
        part2[p] = reduced(p, 0).astype(jnp.bfloat16)
        for ahead in (2, 1, 3):
            stage_copy(p, 1, ahead).start()
    spread(1, gathered(0))
    sent(0)

    for p in range(4):
        part3[p] = reduced(p, 1).astype(jnp.bfloat16)
        for ahead in (2, 1, 3):
            stage_copy(p, 2, ahead).start()
    spread(2, gathered(1))
    sent(1)

    for p in range(4):
        gw_ref[:, p * 128 : (p + 1) * 128] = reduced(p, 2)
    tot_ref[...] = jnp.broadcast_to(
        jnp.sum(gathered(2), axis=1, keepdims=True), (8, 128)
    )

    for ahead in (1, 2, 3):
        for p in range(4):
            stage_copy(p, 2, ahead).wait_send()
        total_axis(2, ahead).wait_send()


def scale_kernel(
    pair_count, items, gh_ref, gw_ref, tot_ref, gh_out, gw_out, loss_out, buf, gw_buf, loss_buf, sem
):
    totals = tot_ref[...]
    weight_total = totals[0:1, :] * (0.5 / math.log(2.0))
    pair_loss = totals[1:2, :] * 0.5
    inverse = float(pair_count) / weight_total
    across = jnp.broadcast_to(jnp.concatenate([inverse] * 16, axis=1), (16, FF))
    gw_buf[...] = gw_ref[...] * (across[:, :D] * (1.0 / items))
    loss_buf[...] = (pair_loss / weight_total)[:, 0:1]
    small = (
        pltpu.make_async_copy(gw_buf, gw_out, sem.at[8]),
        pltpu.make_async_copy(loss_buf, loss_out, sem.at[9]),
    )
    for copy in small:
        copy.start()

    def out(i):
        rows = pl.ds(i * 128, 128)
        return pltpu.make_async_copy(buf.at[rows], gh_out.at[rows], sem.at[i])

    for i in range(8):
        for n in range(8):
            rows = slice(i * 128 + n * 16, i * 128 + (n + 1) * 16)
            buf[rows, :] = (gh_ref[rows, :].astype(jnp.float32) * across).astype(jnp.bfloat16)
        out(i).start()
    for i in range(8):
        out(i).wait()
    for copy in small:
        copy.wait()


def on_device(hidden, weight, stamps, group_ids):
    device_count = lax.axis_size("blk") * lax.axis_size("grp")
    bf, f32 = jnp.bfloat16, jnp.float32
    sem = pltpu.SemaphoreType.DMA
    vm = pltpu.VMEM
    whole = pl.BlockSpec(memory_space=pl.ANY)
    outside = pl.BlockSpec(memory_space=pltpu.HBM)
    local = pl.BlockSpec(memory_space=pltpu.VMEM)
    grad, partial, totals = pl.pallas_call(
        kernel,
        out_shape=(
            pltpu.VMEM((ROWS, FF), bf),
            pltpu.VMEM((16, D), f32),
            pltpu.VMEM((8, 128), f32),
        ),
        in_specs=[outside] * 4,
        out_specs=(local, local, local),
        scratch_shapes=[
            vm((ROWS, FF), bf), vm((FF, D), bf), vm((2, 4, 4, 4, 16, ROWS), bf),
            vm((4, 4, 4, 16, ROWS), bf), vm((4 * ROWS, D), bf),
            vm((2, 8, 128), jnp.int32), vm((3, 2, 8, 128), jnp.int32),
            vm((32, 128), f32), vm((32, 128), f32), vm((32, 128), f32),
            vm((ROWS, 128), f32), vm((ROWS, 128), f32), vm((ROWS, 128), f32),
            vm((ROWS, D), f32), vm((2, ROWS, D), bf), vm((ROWS, 512), bf), vm((ROWS, CHUNK), bf), vm((ROWS, 128), bf),
            vm((2, 8, 128), f32), vm((4, CHUNK, D), f32),
            vm((4, 4, 4, 4, 16, 128), bf), vm((4, 4, 4, 16, 128), bf), vm((4, 4, 16, 128), bf),
            vm((4, 3, 4, 4, 16, 128), bf), vm((4, 3, 4, 16, 128), bf), vm((4, 3, 16, 128), bf),
            vm((4, 8, 128), f32), vm((8, 128), f32), vm((3, 4, 8, 128), f32),
            sem((15,)), sem((3,)), sem((3,)), sem((4,)), sem((4,)),
            sem((2, 8)), sem((2, 8)), sem((2, 4)), sem((2, 4)), sem((2, 2)), sem((2, 2)), sem((4,)), sem((4,)), sem((4,)), sem((4,)),
            sem((4, 3)), sem((4, 3)), sem((4, 3)), sem((4, 3)), sem((4, 3)), sem((4, 3)),
            sem, sem, sem((3, 3)), sem((3, 3)),
        ],
        compiler_params=pltpu.CompilerParams(
            collective_id=0, has_side_effects=True, vmem_limit_bytes=44 << 20
        ),
        cost_estimate=pl.CostEstimate(
            flops=15 * 10**9, bytes_accessed=7 << 20, transcendentals=12 << 20
        ),
    )(*(
        pltpu.with_memory_space_constraint(value, pltpu.HBM)
        for value in (hidden, weight, stamps.reshape(8, 128), group_ids.reshape(8, 128))
    ))
    items = device_count * ROWS
    pair_count = items * (ROWS - 1) // 2 + 3 * items * ROWS // 2
    grad_hidden, grad_weight, loss = pl.pallas_call(
        functools.partial(scale_kernel, pair_count, items),
        out_shape=(
            jax.ShapeDtypeStruct((ROWS, FF), bf),
            jax.ShapeDtypeStruct((16, D), f32),
            jax.ShapeDtypeStruct((1, 1), f32),
        ),
        in_specs=[local, local, local],
        out_specs=(whole, whole, whole),
        scratch_shapes=[vm((ROWS, FF), bf), vm((16, D), f32), vm((1, 1), f32), sem((10,))],
        compiler_params=pltpu.CompilerParams(vmem_limit_bytes=16 << 20),
        cost_estimate=pl.CostEstimate(
            flops=2 << 20, bytes_accessed=4 << 20, transcendentals=0
        ),
    )(grad, partial, totals)
    return grad_hidden, grad_weight, loss[0, 0]


def solution(mesh):
    in_specs = (P(("blk", "grp"), None), P(), P(("blk", "grp")), P(("blk", "grp")))
    out_specs = (P(("blk", "grp"), None), P(("blk", "grp"), None), P())
    return jax.shard_map(
        on_device, mesh=mesh, in_specs=in_specs, out_specs=out_specs, check_vma=False
    )
```
